128 devices in a mesh: wide: 16 (over x_lo, y, core), narrow: 8 (over x_hi, z).
Axes of the slice: x: 4 (x_hi: 2, x_lo: 2; x = x_hi * 2 + x_lo), y: 4, z: 4, core: 2. Of those that a mesh axis runs over, the one named last changes fastest.
Arguments:
- node_features: bfloat16 [131072, 128], P(('wide', 'narrow')), may hold values from -6 to 6
- tile_values: bfloat16 [65536, 128, 128], P(('wide', 'narrow')), may hold values from -0.1875 to 0.1875
- tile_rows: int32 [65536], P(('wide', 'narrow')), may hold values from 0 to 63, as said below
- tile_cols: int32 [65536], P(('wide', 'narrow')), may hold values from 0 to 127, as said below
- tile_count: int32 [128], P(('wide', 'narrow')), may hold values from 64 to 512, as said below
- weight_self: bfloat16 [128, 256], replicated, may hold values from -0.5 to 0.5
- weight_neigh: bfloat16 [128, 256], replicated, may hold values from -0.5 to 0.5
- bias_vector: float32 [256], replicated, may hold values from -3 to 3
- grad_output: bfloat16 [131072, 256], P(('wide', 'narrow')), may hold values from -6 to 6
Outputs:
- node_output: bfloat16 [131072, 256], P(('wide', 'narrow'))
- grad_input: bfloat16 [131072, 128], P(('wide', 'narrow'))
- grad_self: float32 [128, 256], replicated
- grad_neigh: float32 [128, 256], replicated
- grad_bias: float32 [256], replicated
The draws below stay inside these ranges and needn't reach their ends.
Inputs may be any that keep to these rules, and one draw needn't show every extreme that they name: `tile_rows`: each device's 512 slots name distinct tiles in ascending order of row tile, then column tile. `tile_cols`: column tile c lies in the panel of device (c // 8, n) of the column group. `tile_count`: some device has all 512 slots live.
All inputs are finite; a program needn't handle non-finite values.
Results may differ from the reference program's by a relative error of at most 0.029.
Values may be sent and summed in bfloat16 or wider, within the bound.
No kernel may reach another device: no remote copies, remote signals or barrier semaphores. Data moves between devices by JAX's collectives and lax.ppermute only.
A program may use at most 256 MiB of HBM per device.

```python
import jax
import jax.numpy as jnp
from jax import lax

TILE = 128
BLOCKS_DEV = 8
FEAT = 128
HID = 256
TILES_ROW = 8
NODE_DEV = 1024
TILES_DEV = 512
NODES = 131072
N_WIDE = 16
N_NARROW = 8


def tile_cells(key):
    row_tiles = N_NARROW * BLOCKS_DEV
    col_tiles = N_WIDE * BLOCKS_DEV
    devices = N_WIDE * N_NARROW
    keys = jax.random.split(key, devices)

    def one_device(device_key):
        chosen = jax.random.permutation(device_key, row_tiles * col_tiles)[:TILES_DEV]
        return jnp.sort(chosen).astype(jnp.int32)
    cells = jax.vmap(one_device)(keys)
    return (cells // col_tiles, cells % col_tiles)


def draw_tile_rows(key, part):
    rows_index, cols_index = tile_cells(key)
    return rows_index.reshape(-1).astype(jnp.int32)


def draw_tile_cols(key, part):
    rows_index, cols_index = tile_cells(key)
    return cols_index.reshape(-1).astype(jnp.int32)


def draw_tile_count(key, part):
    key = jax.random.fold_in(key, 3)
    devices = N_WIDE * N_NARROW
    lowest = TILES_DEV // 8
    spread = TILES_DEV - lowest
    first_key, second_key = jax.random.split(key)
    raw = jax.random.randint(first_key, (devices,), 0, spread + 1)
    counts = lowest + raw * raw // spread
    fullest = jax.random.randint(second_key, (), 0, devices)
    counts = jnp.where(jnp.arange(devices) == fullest, TILES_DEV, counts)
    return counts.astype(jnp.int32)


def block_levels(stream_key, shape, cuts, smallest, top_value):
    gain = 1.0
    for dim, blocks in cuts:
        heights = jax.random.uniform(jax.random.fold_in(jax.random.fold_in(stream_key, 6), dim), (blocks,), jnp.float32, smallest / len(cuts), top_value / len(cuts))
        gain = gain * jnp.repeat(jnp.exp(heights), shape[dim] // blocks).reshape((-1,) + (1,) * (len(shape) - 1 - dim))
    return gain


def scatter_about(rng, extent, width, reach, cuts=(), dtype=jnp.bfloat16):
    factor_of = block_levels(rng, extent, cuts, -0.22, 0.18) if cuts else 1.0
    array = jax.random.normal(rng, extent, jnp.float32) * width * factor_of
    return jnp.minimum(jnp.maximum(array, -reach), reach).astype(dtype)


def setup_inputs(seed: int = 0) -> dict:
    seeds = jax.random.split(jax.random.key(seed), 10)
    node_features = scatter_about(seeds[0], (NODES, FEAT), 1.0, 6.0, ((0, 128),))
    tile_values = scatter_about(seeds[1], (N_WIDE * N_NARROW * TILES_DEV, TILE, TILE), (TILES_ROW * TILE) ** -0.5, 0.1875, ((0, 128),))
    tile_rows = draw_tile_rows(jax.random.fold_in(seeds[9], 71), 0)
    tile_cols = draw_tile_cols(jax.random.fold_in(seeds[9], 71), 0)
    tile_count = draw_tile_count(jax.random.fold_in(seeds[9], 71), 0)
    weight_self = scatter_about(seeds[5], (FEAT, HID), FEAT ** -0.5, 0.5)
    weight_neigh = scatter_about(seeds[6], (FEAT, HID), FEAT ** -0.5, 0.5)
    bias_vector = scatter_about(seeds[7], (HID,), 0.5, 3.0, (), jnp.float32)
    grad_output = scatter_about(seeds[8], (NODES, HID), 1.0, 6.0, ((0, 128),))
    return {"node_features": node_features, "tile_values": tile_values, "tile_rows": tile_rows, "tile_cols": tile_cols, "tile_count": tile_count, "weight_self": weight_self, "weight_neigh": weight_neigh, "bias_vector": bias_vector, "grad_output": grad_output}


def stripe_tiles(values, rows_index, cols_index, count, source, out_tiles, transpose):
    tile_size = values.shape[1]
    features = source.shape[1]
    present = (jnp.arange(values.shape[0]) < count).astype(jnp.float32)
    blocks = source.reshape(-1, tile_size, features).astype(jnp.float32)
    if transpose:
        picked = blocks[rows_index]
        pattern = "tji,tjf->tif"
        target = cols_index
    else:
        picked = blocks[cols_index]
        pattern = "tij,tjf->tif"
        target = rows_index
    products = jnp.einsum(pattern, values.astype(jnp.float32), picked, precision=lax.Precision.HIGHEST)
    products = products * present[:, None, None]
    summed = jax.ops.segment_sum(products, target, num_segments=out_tiles)
    return summed.reshape(out_tiles * tile_size, features)


def reference(node_features, tile_values, tile_rows, tile_cols, tile_count, weight_self, weight_neigh, bias_vector, grad_output):
    row_tiles = N_NARROW * BLOCKS_DEV
    col_tiles = N_WIDE * BLOCKS_DEV
    stripe_len = N_NARROW * NODE_DEV
    grouped = node_features.reshape(N_WIDE, N_NARROW, NODE_DEV, FEAT)
    values = tile_values.reshape(N_WIDE, N_NARROW, TILES_DEV, TILE, TILE)
    rows_all = tile_rows.reshape(N_WIDE, N_NARROW, TILES_DEV)
    cols_all = tile_cols.reshape(N_WIDE, N_NARROW, TILES_DEV)
    counts = tile_count.reshape(N_WIDE, N_NARROW)

    def forward_stripe(stripe):
        def add_group(column, totals):
            panel = grouped[:, column].reshape(N_WIDE * NODE_DEV, FEAT)
            return totals + stripe_tiles(values[stripe, column], rows_all[stripe, column], cols_all[stripe, column], counts[stripe, column], panel, row_tiles, False)
        return lax.fori_loop(0, N_NARROW, add_group, jnp.zeros((stripe_len, FEAT), jnp.float32))

    aggregate = lax.map(forward_stripe, jnp.arange(N_WIDE)).reshape(NODES, FEAT).astype(jnp.bfloat16)
    preact = jnp.dot(node_features, weight_self, preferred_element_type=jnp.float32)
    preact = preact + jnp.dot(aggregate, weight_neigh, preferred_element_type=jnp.float32) + bias_vector
    sigma = jax.nn.sigmoid(preact)
    node_output = (preact * sigma).astype(jnp.bfloat16)
    grad_pre = (grad_output.astype(jnp.float32) * sigma * (1.0 + preact * (1.0 - sigma))).astype(jnp.bfloat16)
    grad_agg = jnp.dot(grad_pre, weight_neigh.T, preferred_element_type=jnp.float32).astype(jnp.bfloat16)
    scale = float(NODES) ** -0.5
    grad_self = jnp.dot(node_features.T, grad_pre, preferred_element_type=jnp.float32) * scale
    grad_neigh = jnp.dot(aggregate.T, grad_pre, preferred_element_type=jnp.float32) * scale
    grad_bias = jnp.sum(grad_pre.astype(jnp.float32), axis=0) * scale
    agg_stripes = grad_agg.reshape(N_WIDE, stripe_len, FEAT)

    def backward_group(column):
        def add_stripe(stripe, totals):
            return totals + stripe_tiles(values[stripe, column], rows_all[stripe, column], cols_all[stripe, column], counts[stripe, column], agg_stripes[stripe], col_tiles, True)
        return lax.fori_loop(0, N_WIDE, add_stripe, jnp.zeros((N_WIDE * NODE_DEV, FEAT), jnp.float32))

    column_terms = lax.map(backward_group, jnp.arange(N_NARROW))
    column_terms = column_terms.reshape(N_NARROW, N_WIDE, NODE_DEV, FEAT).transpose(1, 0, 2, 3).reshape(NODES, FEAT)
    grad_input = (jnp.dot(grad_pre, weight_self.T, preferred_element_type=jnp.float32) + column_terms).astype(jnp.bfloat16)
    return (node_output, grad_input, grad_self, grad_neigh, grad_bias)
```

```python
import jax
import jax.numpy as jnp
from jax import lax
from jax.experimental import pallas as pl
from jax.experimental.pallas import tpu as pltpu
from jax.sharding import PartitionSpec as P

TILE = 128
X_LO, Y, CORES = 2, 4, 2
X_HI, Z = 2, 4
PANEL = 8
CHUNK = 32
UNROLL = 32
BATCH = 4
SLICE = 32
VMEM_BYTES = 56 * 1024 * 1024
RELATIVE = [(dx, dy) for dx in (0, 1) for dy in range(4)]


def wide_index(w, dx, dy, dc):
    return ((w >> 3) ^ dx) * 8 + ((((w >> 1) & 3) + dy) & 3) * 2 + ((w & 1) ^ dc)


def narrow_index(n, dx, dz):
    return ((n >> 2) ^ dx) * 4 + (((n & 3) + dz) & 3)


def from_wide(x, dx, dy, dc):
    return lax.ppermute(x, "wide", [(wide_index(w, dx, dy, dc), w) for w in range(16)])


def from_narrow(x, dx, dz):
    return lax.ppermute(x, "narrow", [(narrow_index(n, dx, dz), n) for n in range(8)])


def gather_ring(x, fetch):
    got = {(0, 0): x}
    got[0, 1] = fetch(x, 0, 1)
    got[0, 3] = fetch(x, 0, 3)
    got[1, 0] = fetch(x, 1, 0)
    got[0, 2] = fetch(got[0, 1], 0, 1)
    got[1, 1] = fetch(got[1, 0], 0, 1)
    got[1, 3] = fetch(got[1, 0], 0, 3)
    got[1, 2] = fetch(got[0, 2], 1, 0)
    return [got[key] for key in RELATIVE]


def load_tiles(tiles_hbm, tiles, sems, count):
    chunks = tiles_hbm.shape[0] // CHUNK
    copies = [
        pltpu.make_async_copy(
            tiles_hbm.at[pl.ds(k * CHUNK, CHUNK)], tiles.at[pl.ds(k * CHUNK, CHUNK)], sems.at[k]
        )
        for k in range(chunks)
    ]
    for k, copy in enumerate(copies):

        @pl.when(k * CHUNK < count)
        def _():
            copy.start()


def wait_chunk(tiles_hbm, tiles, sems, k):
    span = pl.ds(k * CHUNK, CHUNK)
    pltpu.make_async_copy(tiles_hbm.at[span], tiles.at[span], sems.at[k]).wait()


def plan_kernel(meta, rows, pairs, total):
    slots, trash = rows.shape[0], meta[3]
    count = meta[0]

    def place(state):
        s, k = state
        row = rows[s]
        after = jnp.minimum(s + 1, slots - 1)
        both = (s + 1 < count) & (rows[after] == row)
        pairs[0, k] = row
        pairs[1, k] = s
        pairs[2, k] = jnp.where(both, s + 1, slots)
        return s + 1 + both.astype(jnp.int32), k + 1

    _, k = lax.while_loop(lambda state: state[0] < count, place, (jnp.int32(0), jnp.int32(0)))
    total[0] = (k + UNROLL - 1) // UNROLL
    for u in range(UNROLL):
        pairs[0, k + u] = trash
        pairs[1, k + u] = slots
        pairs[2, k + u] = slots


def visit_pairs(count, total, pairs, visit, tiles_hbm, tiles, sems):
    last = (count + CHUNK - 1) // CHUNK - 1

    def group(i, arrived):
        needed = jnp.minimum((pairs[1, i * UNROLL + UNROLL - 1] + 1) // CHUNK, last)

        def wait(k, carry):
            wait_chunk(tiles_hbm, tiles, sems, k)
            return carry

        lax.fori_loop(arrived, needed + 1, wait, 0)
        visit([[pairs[j, i * UNROLL + u] for j in range(3)] for u in range(UNROLL)])
        return needed + 1

    lax.fori_loop(0, total[0], group, jnp.int32(0))


def forward_kernel(meta, cols, pairs, total, tiles_hbm, *refs):
    panels_hbm, outs = refs[:16], refs[16:24]
    panels, tiles, acc, panel_sems, tile_sems = refs[24:]
    count, w, n = meta[0], meta[1], meta[2]
    copies = []
    for k in range(16):
        dx, dy = RELATIVE[k % 8]
        owner = wide_index(w, dx, dy, k // 8)
        copies.append(
            pltpu.make_async_copy(
                panels_hbm[k], panels.at[pl.ds(owner * 1024, 1024)], panel_sems.at[k]
            )
        )
    for copy in copies:
        copy.start()
    load_tiles(tiles_hbm, tiles, tile_sems, count)
    acc[...] = jnp.zeros_like(acc)
    tiles[tiles.shape[0] - 1] = jnp.zeros(tiles.shape[1:], tiles.dtype)
    spare = pl.ds(panels.shape[0] - TILE, TILE)
    panels[spare, :] = jnp.zeros((TILE, panels.shape[1]), panels.dtype)
    for copy in copies:
        copy.wait()

    def panel(s):
        column = pl.multiple_of(cols[s] * TILE, TILE)
        return panels[pl.ds(column, TILE), :]

    def visit(group):
        for part in range(0, UNROLL, BATCH):
            products = []
            for row, first, second in group[part : part + BATCH]:
                left = jnp.concatenate([tiles[first], tiles[second]], axis=1)
                right = jnp.concatenate([panel(first), panel(second)], axis=0)
                products.append(jnp.dot(left, right, preferred_element_type=jnp.float32))
            for (row, _, _), product in zip(group[part : part + BATCH], products):
                acc[row] += product

    visit_pairs(count, total, pairs, visit, tiles_hbm, tiles, tile_sems)
    for k, (dx, dz) in enumerate(RELATIVE):
        owner = narrow_index(n, dx, dz)
        block = acc[pl.ds(owner * PANEL, PANEL)]
        outs[k][...] = block.reshape(PANEL * TILE, -1).astype(jnp.bfloat16)


def dense_kernel(
    own, r1, r2, r3, r4, r5, r6, r7, x, ws, wn, bias, grad, output, agg_out, pre_out, back_out
):
    agg = own[...].astype(jnp.float32)
    for r in (r1, r2, r3, r4, r5, r6, r7):
        agg = agg + r[...].astype(jnp.float32)
    agg = agg.astype(jnp.bfloat16)
    agg_out[...] = agg
    preact = jnp.dot(x[...], ws[...], preferred_element_type=jnp.float32)
    preact = preact + jnp.dot(agg, wn[...], preferred_element_type=jnp.float32) + bias[...]
    sigma = jax.nn.sigmoid(preact)
    output[...] = (preact * sigma).astype(jnp.bfloat16)
    pre = grad[...].astype(jnp.float32) * sigma * (1.0 + preact * (1.0 - sigma))
    pre = pre.astype(jnp.bfloat16)
    pre_out[...] = pre
    back = lax.dot_general(
        wn[...], pre, (((1,), (1,)), ((), ())), preferred_element_type=jnp.float32
    )
    back = back.astype(jnp.bfloat16)
    for k in range(back_out.shape[0]):
        back_out[k] = back[:, k * TILE : (k + 1) * TILE]


def weight_kernel(scale, meta, x, agg, pre, ws, far, near, self_term):
    rows = (((0,), (0,)), ((), ()))
    n = meta[2]
    block = pre[...]
    half = [
        scale * lax.dot_general(v[...], block, rows, preferred_element_type=jnp.float32)
        for v in (x, agg)
    ]
    mine = (n >> 2) == 0
    total = scale * jnp.sum(block.astype(jnp.float32), axis=0, keepdims=True)
    total = jnp.broadcast_to(total, (8, total.shape[1]))
    for out, grads in (
        (near, jnp.where(mine, half[0], half[1])),
        (far, jnp.where(mine, half[1], half[0])),
    ):
        for z in range(Z):
            place = (z - n) & 3
            out[place, :SLICE] = grads[z * SLICE : (z + 1) * SLICE]
            out[place, SLICE:] = total
    self_term[...] = lax.dot_general(
        block, ws[...], (((1,), (1,)), ((), ())), preferred_element_type=jnp.float32
    )


def assemble_kernel(meta, s0, s1, s2, s3, other, grad_self, grad_neigh, grad_bias):
    n = meta[2]
    mine = (n >> 2) == 0
    grad_bias[...] = s0[SLICE : SLICE + 1, :]
    for dz, s in enumerate((s0, s1, s2, s3)):
        place = pl.ds(pl.multiple_of(((n + dz) & 3) * SLICE, SLICE), SLICE)
        here, there = s[:SLICE, :], other[dz, :SLICE, :]
        grad_self[place, :] = jnp.where(mine, here, there)
        grad_neigh[place, :] = jnp.where(mine, there, here)


def backward_kernel(meta, cols, pairs, total, tiles_hbm, *refs):
    grads_hbm, (swap, keep) = refs[:8], refs[8:10]
    grads, tiles, acc, grad_sems, tile_sems = refs[10:]
    count, w, n = meta[0], meta[1], meta[2]
    copies = []
    for k, (dx, dz) in enumerate(RELATIVE):
        owner = narrow_index(n, dx, dz)
        copies.append(
            pltpu.make_async_copy(
                grads_hbm[k], grads.at[pl.ds(owner * PANEL, PANEL)], grad_sems.at[k]
            )
        )
    for copy in copies:
        copy.start()
    load_tiles(tiles_hbm, tiles, tile_sems, count)
    acc[...] = jnp.zeros_like(acc)
    tiles[tiles.shape[0] - 1] = jnp.zeros(tiles.shape[1:], tiles.dtype)
    grads[grads.shape[0] - 1] = jnp.zeros(grads.shape[1:], grads.dtype)
    for copy in copies:
        copy.wait()

    def visit(group):
        for part in range(0, UNROLL, BATCH):
            products = []
            for row, first, second in group[part : part + BATCH]:
                right = jnp.concatenate([tiles[first], tiles[second]], axis=1)
                products.append(jnp.dot(grads[row], right, preferred_element_type=jnp.float32))
            for (_, first, second), product in zip(group[part : part + BATCH], products):
                acc[cols[first]] += product[:, :TILE]
                acc[cols[second]] += product[:, TILE:]

    visit_pairs(count, total, pairs, visit, tiles_hbm, tiles, tile_sems)
    for k, (dx, dy) in enumerate(RELATIVE):
        for dc, out in ((0, keep), (1, swap)):
            owner = wide_index(w, dx, dy, dc)
            out[k] = acc[pl.ds(owner * PANEL, PANEL)].astype(jnp.bfloat16)


def final_kernel(keep, swapped, r1, r2, r3, r4, r5, r6, r7, self_term, out):
    for j in range(r1.shape[0]):
        total = keep[0, j].astype(jnp.float32) + swapped[0, j].astype(jnp.float32)
        for r in (r1, r2, r3, r4, r5, r6, r7):
            total = total + r[j].astype(jnp.float32)
        rows = pl.ds(j * TILE, TILE)
        out[rows, :] = (self_term[rows, :] + total.T).astype(jnp.bfloat16)


def local(
    node_features,
    tile_values,
    tile_rows,
    tile_cols,
    tile_count,
    weight_self,
    weight_neigh,
    bias_vector,
    grad_output,
):
    slots = tile_values.shape[0]
    own_nodes, features = node_features.shape
    hidden = weight_self.shape[1]
    wide_count = lax.axis_size("wide")
    narrow_count = lax.axis_size("narrow")
    row_tiles = narrow_count * PANEL
    col_tiles = wide_count * PANEL
    w, n = lax.axis_index("wide"), lax.axis_index("narrow")
    meta = jnp.stack([tile_count[0], w.astype(jnp.int32), n.astype(jnp.int32), row_tiles])
    dead = jnp.full((1,), col_tiles, jnp.int32)
    cols = jnp.concatenate([tile_cols, dead])
    smem = pl.BlockSpec(memory_space=pltpu.SMEM)
    hbm = pl.BlockSpec(memory_space=pl.ANY)
    vmem = pl.BlockSpec(memory_space=pltpu.VMEM)
    scale = float(own_nodes * wide_count * narrow_count) ** (-0.5)
    bf16, f32 = jnp.bfloat16, jnp.float32
    tile_dots = pl.CostEstimate(
        flops=2 * slots * TILE * TILE * features,
        bytes_accessed=2 * slots * TILE * TILE + 6 * 1024 * 1024,
        transcendentals=0,
    )

    with jax.named_scope("gather_features"):
        same_core = gather_ring(node_features, lambda v, dx, dy: from_wide(v, dx, dy, 0))
        other_core = [from_wide(v, 0, 0, 1) for v in same_core]

    with jax.named_scope("plan"):
        pairs, total = pl.pallas_call(
            plan_kernel,
            out_shape=[
                jax.ShapeDtypeStruct((3, (slots + row_tiles) // 2 + UNROLL), jnp.int32),
                jax.ShapeDtypeStruct((1,), jnp.int32),
            ],
            in_specs=[smem] * 2,
            out_specs=[smem] * 2,
            name="plan",
        )(meta, tile_rows)

    with jax.named_scope("aggregate"):
        partial = pl.pallas_call(
            forward_kernel,
            out_shape=[jax.ShapeDtypeStruct((own_nodes, features), bf16)] * 8,
            in_specs=[smem] * 4 + [hbm] * 17,
            out_specs=[vmem] * 8,
            scratch_shapes=[
                pltpu.VMEM(((col_tiles + 1) * TILE, features), bf16),
                pltpu.VMEM((slots + 1, TILE, TILE), bf16),
                pltpu.VMEM((row_tiles + 1, TILE, features), f32),
                pltpu.SemaphoreType.DMA((16,)),
                pltpu.SemaphoreType.DMA((slots // CHUNK,)),
            ],
            compiler_params=pltpu.CompilerParams(vmem_limit_bytes=VMEM_BYTES),
            cost_estimate=tile_dots,
            name="aggregate",
        )(meta, cols, pairs, total, tile_values, *same_core, *other_core)

    with jax.named_scope("scatter_aggregate"):
        received = [
            from_narrow(partial[k], dx, -dz & 3)
            for k, (dx, dz) in enumerate(RELATIVE)
            if k > 0
        ]

    block = own_nodes // 2
    node_spec = pl.BlockSpec((block, features), lambda i: (i, 0))
    hid_spec = pl.BlockSpec((block, hidden), lambda i: (i, 0))
    weight_spec = pl.BlockSpec((features, hidden), lambda i: (0, 0))
    piece_spec = pl.BlockSpec((block // TILE, features, TILE), lambda i: (i, 0, 0))
    with jax.named_scope("dense"):
        output, own_agg, grad_pre, back = pl.pallas_call(
            dense_kernel,
            grid=(own_nodes // block,),
            out_shape=[
                jax.ShapeDtypeStruct((own_nodes, hidden), bf16),
                jax.ShapeDtypeStruct((own_nodes, features), bf16),
                jax.ShapeDtypeStruct((own_nodes, hidden), bf16),
                jax.ShapeDtypeStruct((PANEL, features, TILE), bf16),
            ],
            in_specs=[node_spec] * 9
            + [weight_spec, weight_spec, pl.BlockSpec((1, hidden), lambda i: (0, 0)), hid_spec],
            out_specs=[hid_spec, node_spec, hid_spec, piece_spec],
            compiler_params=pltpu.CompilerParams(vmem_limit_bytes=VMEM_BYTES),
            name="dense",
        )(
            partial[0],
            *received,
            node_features,
            weight_self,
            weight_neigh,
            bias_vector.reshape(1, hidden),
            grad_output,
        )

    with jax.named_scope("gather_gradients"):
        grads = gather_ring(back, from_narrow)

    with jax.named_scope("weight_gradients"):
        slices = jax.ShapeDtypeStruct((Z, SLICE + 8, hidden), f32)
        far, near, self_term = pl.pallas_call(
            lambda *refs: weight_kernel(scale, *refs),
            out_shape=[slices, slices, jax.ShapeDtypeStruct((own_nodes, features), f32)],
            in_specs=[smem] + [vmem] * 4,
            out_specs=[vmem] * 3,
            compiler_params=pltpu.CompilerParams(vmem_limit_bytes=VMEM_BYTES),
            cost_estimate=pl.CostEstimate(
                flops=6 * own_nodes * features * hidden,
                bytes_accessed=2 * 1024 * 1024,
                transcendentals=0,
            ),
            name="weight_gradients",
        )(meta, node_features, own_agg, grad_pre, weight_self)
        near = near + from_narrow(far, 1, 0)
        part = near[0] + sum(from_narrow(near[dz], 0, -dz & 3) for dz in (1, 2, 3))
        grads[-1], part = lax.optimization_barrier((grads[-1], part))
        part = part + sum(from_wide(part, dx, 0, dc) for dx, dc in ((0, 1), (1, 0), (1, 1)))
        part = part + sum(from_wide(part, 0, dy, 0) for dy in (1, 2, 3))

    with jax.named_scope("column_gradients"):
        pieces = jax.ShapeDtypeStruct((8, PANEL, features, TILE), bf16)
        swap, keep = pl.pallas_call(
            backward_kernel,
            out_shape=[pieces, pieces],
            in_specs=[smem] * 4 + [hbm] * 9,
            out_specs=[vmem] * 2,
            scratch_shapes=[
                pltpu.VMEM((row_tiles + 1, features, TILE), bf16),
                pltpu.VMEM((slots + 1, TILE, TILE), bf16),
                pltpu.VMEM((col_tiles + 1, features, TILE), f32),
                pltpu.SemaphoreType.DMA((8,)),
                pltpu.SemaphoreType.DMA((slots // CHUNK,)),
            ],
            compiler_params=pltpu.CompilerParams(vmem_limit_bytes=VMEM_BYTES),
            cost_estimate=tile_dots,
            name="column_gradients",
        )(meta, cols, pairs, total, tile_values, *grads)

    with jax.named_scope("scatter_gradients"):
        swapped = from_wide(swap, 0, 0, 1)
        column = []
        for k, (dx, dy) in enumerate(RELATIVE):
            if k > 0:
                pair = (keep[k].astype(f32) + swapped[k].astype(f32)).astype(bf16)
                column.append(from_wide(pair, dx, -dy & 3, 0))

    with jax.named_scope("spread_weight_gradients"):
        quarters = [part] + [from_narrow(part, 0, dz) for dz in (1, 2, 3)]
        other = from_narrow(jnp.stack(quarters), 1, 0)
        grad_self, grad_neigh, grad_bias = pl.pallas_call(
            assemble_kernel,
            out_shape=[
                jax.ShapeDtypeStruct((features, hidden), f32),
                jax.ShapeDtypeStruct((features, hidden), f32),
                jax.ShapeDtypeStruct((1, hidden), f32),
            ],
            in_specs=[smem] + [vmem] * 5,
            out_specs=[vmem] * 3,
            name="assemble",
        )(meta, *quarters, other)

    with jax.named_scope("grad_input"):
        first_spec = pl.BlockSpec((1, block // TILE, features, TILE), lambda i: (0, i, 0, 0))
        grad_input = pl.pallas_call(
            final_kernel,
            grid=(own_nodes // block,),
            out_shape=jax.ShapeDtypeStruct((own_nodes, features), bf16),
            in_specs=[first_spec] * 2 + [piece_spec] * 7 + [node_spec],
            out_specs=node_spec,
            compiler_params=pltpu.CompilerParams(vmem_limit_bytes=VMEM_BYTES),
            name="grad_input",
        )(keep, swapped, *column, self_term)
    return (output, grad_input, grad_self, grad_neigh, grad_bias[0])


def solution(mesh):
    placed = (
        P(("wide", "narrow"), None),
        P(("wide", "narrow"), None, None),
        P(("wide", "narrow")),
        P(("wide", "narrow")),
        P(("wide", "narrow")),
        P(),
        P(),
        P(),
        P(("wide", "narrow"), None),
    )
    return jax.shard_map(
        local,
        mesh=mesh,
        in_specs=placed,
        out_specs=(P(("wide", "narrow"), None), P(("wide", "narrow"), None), P(), P(), P()),
        check_vma=False,
    )
```

```python
import jax
import jax.numpy as jnp
from jax import lax
from jax.experimental import pallas as pl
from jax.experimental.pallas import tpu as pltpu
from jax.sharding import PartitionSpec as P

TILE = 128
X_LO, Y, CORES = 2, 4, 2
X_HI, Z = 2, 4
PANEL = 8
CHUNK = 32
UNROLL = 32
BATCH = 4
SLICE = 64
STEPS = ((), (4, 6, 2), (1, 3, 5, 7))
VMEM_BYTES = 56 * 1024 * 1024
RELATIVE = [(dx, dy) for dx in (0, 1) for dy in range(4)]


def wide_index(w, dx, dy, dc):
    return ((w >> 3) ^ dx) * 8 + ((((w >> 1) & 3) + dy) & 3) * 2 + ((w & 1) ^ dc)


def narrow_index(n, dx, dz):
    return ((n >> 2) ^ dx) * 4 + (((n & 3) + dz) & 3)


def from_wide(x, dx, dy, dc):
    return lax.ppermute(x, "wide", [(wide_index(w, dx, dy, dc), w) for w in range(16)])


def from_narrow(x, dx, dz):
    return lax.ppermute(x, "narrow", [(narrow_index(n, dx, dz), n) for n in range(8)])


def gather_ring(x, fetch, together):
    first = [(1, 0), (0, 2), (0, 1), (0, 3)]
    got = dict(zip(first, together([fetch(x, *key) for key in first])))
    got[0, 0] = x
    got[1, 1] = fetch(got[1, 0], 0, 1)
    got[1, 3] = fetch(got[1, 0], 0, 3)
    got[1, 2] = fetch(got[0, 2], 1, 0)
    return [got[key] for key in RELATIVE]


def load_tiles(tiles_hbm, tiles, sems, count):
    chunks = tiles_hbm.shape[0] // CHUNK
    copies = [
        pltpu.make_async_copy(
            tiles_hbm.at[pl.ds(k * CHUNK, CHUNK)], tiles.at[pl.ds(k * CHUNK, CHUNK)], sems.at[k]
        )
        for k in range(chunks)
    ]
    for k, copy in enumerate(copies):

        @pl.when(k * CHUNK < count)
        def _():
            copy.start()


def wait_chunk(tiles_hbm, tiles, sems, k):
    span = pl.ds(k * CHUNK, CHUNK)
    pltpu.make_async_copy(tiles_hbm.at[span], tiles.at[span], sems.at[k]).wait()


def plan_kernel(meta, rows, pairs, total):
    slots, trash = rows.shape[0], meta[3]
    count = meta[0]

    def place(state):
        s, k = state
        row = rows[s]
        after = jnp.minimum(s + 1, slots - 1)
        both = (s + 1 < count) & (rows[after] == row)
        pairs[0, k] = row
        pairs[1, k] = s
        pairs[2, k] = jnp.where(both, s + 1, slots)
        return s + 1 + both.astype(jnp.int32), k + 1

    _, k = lax.while_loop(lambda state: state[0] < count, place, (jnp.int32(0), jnp.int32(0)))
    total[0] = (k + UNROLL - 1) // UNROLL
    for u in range(UNROLL):
        pairs[0, k + u] = trash
        pairs[1, k + u] = slots
        pairs[2, k + u] = slots


def visit_pairs(count, total, pairs, visit, tiles_hbm, tiles, sems):
    last = (count + CHUNK - 1) // CHUNK - 1

    def group(i, arrived):
        needed = jnp.minimum((pairs[1, i * UNROLL + UNROLL - 1] + 1) // CHUNK, last)

        def wait(k, carry):
            wait_chunk(tiles_hbm, tiles, sems, k)
            return carry

        lax.fori_loop(arrived, needed + 1, wait, 0)
        visit([[pairs[j, i * UNROLL + u] for j in range(3)] for u in range(UNROLL)])
        return needed + 1

    lax.fori_loop(0, total[0], group, jnp.int32(0))


def forward_kernel(meta, cols, pairs, total, tiles_hbm, *refs):
    panels_hbm, outs = refs[:16], refs[16:24]
    panels, tiles, acc, staged, panel_sems, tile_sems, out_sems = refs[24:]
    count, w, n = meta[0], meta[1], meta[2]
    copies = []
    for k in range(16):
        dx, dy = RELATIVE[k % 8]
        owner = wide_index(w, dx, dy, k // 8)
        copies.append(
            pltpu.make_async_copy(
                panels_hbm[k], panels.at[pl.ds(owner * 1024, 1024)], panel_sems.at[k]
            )
        )
    for copy in copies:
        copy.start()
    load_tiles(tiles_hbm, tiles, tile_sems, count)
    acc[...] = jnp.zeros_like(acc)
    tiles[tiles.shape[0] - 1] = jnp.zeros(tiles.shape[1:], tiles.dtype)
    for copy in copies:
        copy.wait()

    def panel(s):
        column = pl.multiple_of(cols[jnp.minimum(s, cols.shape[0] - 1)] * TILE, TILE)
        return panels[pl.ds(column, TILE), :]

    def visit(group):
        for part in range(0, UNROLL, BATCH):
            products = []
            for row, first, second in group[part : part + BATCH]:
                left = jnp.concatenate([tiles[first], tiles[second]], axis=1)
                right = jnp.concatenate([panel(first), panel(second)], axis=0)
                products.append(jnp.dot(left, right, preferred_element_type=jnp.float32))
            for (row, _, _), product in zip(group[part : part + BATCH], products):
                acc[row] += product

    visit_pairs(count, total, pairs, visit, tiles_hbm, tiles, tile_sems)
    for k, (dx, dz) in enumerate(RELATIVE):
        owner = narrow_index(n, dx, dz)
        block = acc[pl.ds(owner * PANEL, PANEL)]
        staged[k] = block.reshape(PANEL * TILE, -1).astype(jnp.bfloat16)
        pltpu.make_async_copy(staged.at[k], outs[k], out_sems.at[k]).start()
    for k in range(8):
        pltpu.make_async_copy(staged.at[k], outs[k], out_sems.at[k]).wait()


def dense_kernel(
    own, r1, r2, r3, r4, r5, r6, r7, x, ws, wn, bias, grad, output, agg_out, pre_out, back_out
):
    agg = own[...].astype(jnp.float32)
    for r in (r1, r2, r3, r4, r5, r6, r7):
        agg = agg + r[...].astype(jnp.float32)
    agg = agg.astype(jnp.bfloat16)
    agg_out[...] = agg
    preact = jnp.dot(x[...], ws[...], preferred_element_type=jnp.float32)
    preact = preact + jnp.dot(agg, wn[...], preferred_element_type=jnp.float32) + bias[...]
    sigma = jax.nn.sigmoid(preact)
    output[...] = (preact * sigma).astype(jnp.bfloat16)
    pre = grad[...].astype(jnp.float32) * sigma * (1.0 + preact * (1.0 - sigma))
    pre = pre.astype(jnp.bfloat16)
    pre_out[...] = pre
    back = lax.dot_general(
        wn[...], pre, (((1,), (1,)), ((), ())), preferred_element_type=jnp.float32
    )
    back = back.astype(jnp.bfloat16)
    for k in range(back_out.shape[0]):
        back_out[k] = back[:, k * TILE : (k + 1) * TILE]


def weight_kernel(scale, meta, x, agg, pre, ws, slices, self_term):
    rows = (((0,), (0,)), ((), ()))
    n = meta[2]
    block = pre[...]
    total = scale * jnp.sum(block.astype(jnp.float32), axis=0, keepdims=True)
    total = jnp.broadcast_to(total, (8, total.shape[1]))
    for j, left in enumerate((x, agg)):
        grads = scale * lax.dot_general(left[...], block, rows, preferred_element_type=jnp.float32)
        for k in range(2):
            place = (2 * j + k - n) & 3
            slices[place, :SLICE] = grads[k * SLICE : (k + 1) * SLICE]
            slices[place, SLICE:] = total
    self_term[...] = lax.dot_general(
        block, ws[...], (((1,), (1,)), ((), ())), preferred_element_type=jnp.float32
    )


def backward_kernel(meta, cols, pairs, total, tiles_hbm, *refs):
    grads_hbm, (swap, keep) = refs[:8], refs[8:10]
    grads, tiles, acc, staged, grad_sems, tile_sems, out_sems = refs[10:]
    count, w, n = meta[0], meta[1], meta[2]
    copies = []
    for k, (dx, dz) in enumerate(RELATIVE):
        owner = narrow_index(n, dx, dz)
        copies.append(
            pltpu.make_async_copy(
                grads_hbm[k], grads.at[pl.ds(owner * PANEL, PANEL)], grad_sems.at[k]
            )
        )
    for copy in copies:
        copy.start()
    load_tiles(tiles_hbm, tiles, tile_sems, count)
    acc[...] = jnp.zeros_like(acc)
    tiles[tiles.shape[0] - 1] = jnp.zeros(tiles.shape[1:], tiles.dtype)
    grads[grads.shape[0] - 1] = jnp.zeros(grads.shape[1:], grads.dtype)
    for copy in copies:
        copy.wait()

    def visit(group):
        for part in range(0, UNROLL, BATCH):
            products = []
            for row, first, second in group[part : part + BATCH]:
                right = jnp.concatenate([tiles[first], tiles[second]], axis=1)
                products.append(jnp.dot(grads[row], right, preferred_element_type=jnp.float32))
            for (_, first, second), product in zip(group[part : part + BATCH], products):
                last = cols.shape[0] - 1
                acc[cols[jnp.minimum(first, last)]] += product[:, :TILE]
                acc[cols[jnp.minimum(second, last)]] += product[:, TILE:]

    visit_pairs(count, total, pairs, visit, tiles_hbm, tiles, tile_sems)
    outs = ((1, swap), (0, keep))
    for dc, out in outs:
        for k, (dx, dy) in enumerate(RELATIVE):
            owner = wide_index(w, dx, dy, dc)
            staged[dc, k] = acc[pl.ds(owner * PANEL, PANEL)].astype(jnp.bfloat16)
            pltpu.make_async_copy(staged.at[dc, k], out.at[k], out_sems.at[dc, k]).start()
    for dc, out in outs:
        for k in range(8):
            pltpu.make_async_copy(staged.at[dc, k], out.at[k], out_sems.at[dc, k]).wait()


def final_kernel(
    meta, keep, swapped, r1, r2, r3, r4, r5, r6, r7, self_term, s0, s1, s2, s3, *outs
):
    out, grad_self, grad_neigh, grad_bias = outs
    for j in range(r1.shape[0]):
        total = keep[0, j].astype(jnp.float32) + swapped[0, j].astype(jnp.float32)
        for r in (r1, r2, r3, r4, r5, r6, r7):
            total = total + r[j].astype(jnp.float32)
        rows = pl.ds(j * TILE, TILE)
        out[rows, :] = (self_term[rows, :] + total.T).astype(jnp.bfloat16)

    @pl.when(pl.program_id(0) == 0)
    def _():
        grad_bias[...] = s0[SLICE : SLICE + 1, :]
        for dz, s in enumerate((s0, s1, s2, s3)):
            place = (meta[2] + dz) & 3
            rows = pl.ds(pl.multiple_of((place & 1) * SLICE, SLICE), SLICE)

            @pl.when(place < 2)
            def _():
                grad_self[rows, :] = s[:SLICE, :]

            @pl.when(place >= 2)
            def _():
                grad_neigh[rows, :] = s[:SLICE, :]


def local(
    node_features,
    tile_values,
    tile_rows,
    tile_cols,
    tile_count,
    weight_self,
    weight_neigh,
    bias_vector,
    grad_output,
):
    slots = tile_values.shape[0]
    own_nodes, features = node_features.shape
    hidden = weight_self.shape[1]
    wide_count = lax.axis_size("wide")
    narrow_count = lax.axis_size("narrow")
    row_tiles = narrow_count * PANEL
    col_tiles = wide_count * PANEL
    w, n = lax.axis_index("wide"), lax.axis_index("narrow")
    meta = jnp.stack([tile_count[0], w.astype(jnp.int32), n.astype(jnp.int32), row_tiles])
    smem = pl.BlockSpec(memory_space=pltpu.SMEM)
    hbm = pl.BlockSpec(memory_space=pl.ANY)
    vmem = pl.BlockSpec(memory_space=pltpu.VMEM)
    scale = float(own_nodes * wide_count * narrow_count) ** (-0.5)
    bf16, f32 = jnp.bfloat16, jnp.float32
    tile_dots = pl.CostEstimate(
        flops=2 * slots * TILE * TILE * features,
        bytes_accessed=2 * slots * TILE * TILE + 6 * 1024 * 1024,
        transcendentals=0,
    )

    with jax.named_scope("plan"):
        pairs, total = pl.pallas_call(
            plan_kernel,
            out_shape=[
                jax.ShapeDtypeStruct((3, (slots + row_tiles) // 2 + UNROLL), jnp.int32),
                jax.ShapeDtypeStruct((1,), jnp.int32),
            ],
            in_specs=[smem] * 2,
            out_specs=[smem] * 2,
            name="plan",
        )(meta, tile_rows)

    def after_plan(blocks):
        return lax.optimization_barrier((*blocks, total))[:-1]

    with jax.named_scope("gather_features"):
        same_core = gather_ring(
            node_features, lambda v, dx, dy: from_wide(v, dx, dy, 0), after_plan
        )
        other_core = [from_wide(v, 0, 0, 1) for v in same_core]

    with jax.named_scope("aggregate"):
        partial = pl.pallas_call(
            forward_kernel,
            out_shape=[jax.ShapeDtypeStruct((own_nodes, features), bf16)] * 8,
            in_specs=[smem] * 4 + [hbm] * 17,
            out_specs=[hbm] * 8,
            scratch_shapes=[
                pltpu.VMEM((col_tiles * TILE, features), bf16),
                pltpu.VMEM((slots + 1, TILE, TILE), bf16),
                pltpu.VMEM((row_tiles + 1, TILE, features), f32),
                pltpu.VMEM((8, own_nodes, features), bf16),
                pltpu.SemaphoreType.DMA((16,)),
                pltpu.SemaphoreType.DMA((slots // CHUNK,)),
                pltpu.SemaphoreType.DMA((8,)),
            ],
            compiler_params=pltpu.CompilerParams(vmem_limit_bytes=VMEM_BYTES),
            cost_estimate=tile_dots,
            name="aggregate",
        )(meta, tile_cols, pairs, total, tile_values, *same_core, *other_core)

    with jax.named_scope("scatter_aggregate"):
        received = [from_narrow(partial[k], RELATIVE[k][0], -k & 3) for k in (6, 4, 2, 5, 7, 1, 3)]

    block = own_nodes // 2
    node_spec = pl.BlockSpec((block, features), lambda i: (i, 0))
    hid_spec = pl.BlockSpec((block, hidden), lambda i: (i, 0))
    weight_spec = pl.BlockSpec((features, hidden), lambda i: (0, 0))
    piece_spec = pl.BlockSpec((block // TILE, features, TILE), lambda i: (i, 0, 0))
    with jax.named_scope("dense"):
        output, own_agg, grad_pre, back = pl.pallas_call(
            dense_kernel,
            grid=(own_nodes // block,),
            out_shape=[
                jax.ShapeDtypeStruct((own_nodes, hidden), bf16),
                jax.ShapeDtypeStruct((own_nodes, features), bf16),
                jax.ShapeDtypeStruct((own_nodes, hidden), bf16),
                jax.ShapeDtypeStruct((PANEL, features, TILE), bf16),
            ],
            in_specs=[node_spec] * 9
            + [weight_spec, weight_spec, pl.BlockSpec((1, hidden), lambda i: (0, 0)), hid_spec],
            out_specs=[hid_spec, node_spec, hid_spec, piece_spec],
            compiler_params=pltpu.CompilerParams(vmem_limit_bytes=VMEM_BYTES),
            name="dense",
        )(
            partial[0],
            *received,
            node_features,
            weight_self,
            weight_neigh,
            bias_vector.reshape(1, hidden),
            grad_output,
        )

    with jax.named_scope("weight_gradients"):
        slices, self_term = pl.pallas_call(
            lambda *refs: weight_kernel(scale, *refs),
            out_shape=[
                jax.ShapeDtypeStruct((Z, SLICE + 8, hidden), f32),
                jax.ShapeDtypeStruct((own_nodes, features), f32),
            ],
            in_specs=[smem] + [vmem] * 4,
            out_specs=[vmem] * 2,
            compiler_params=pltpu.CompilerParams(vmem_limit_bytes=VMEM_BYTES),
            cost_estimate=pl.CostEstimate(
                flops=6 * own_nodes * features * hidden,
                bytes_accessed=2 * 1024 * 1024,
                transcendentals=0,
            ),
            name="weight_gradients",
        )(meta, node_features, own_agg, grad_pre, weight_self)

        part = slices[0] + sum(from_narrow(slices[dz], 0, -dz & 3) for dz in (1, 2, 3))

    with jax.named_scope("gather_gradients"):
        grads = gather_ring(back, from_narrow, lax.optimization_barrier)
        *grads, part = lax.optimization_barrier((*grads, part))

    with jax.named_scope("column_gradients"):
        pieces = jax.ShapeDtypeStruct((8, PANEL, features, TILE), bf16)
        swap, keep = pl.pallas_call(
            backward_kernel,
            out_shape=[pieces, pieces],
            in_specs=[smem] * 4 + [hbm] * 9,
            out_specs=[hbm] * 2,
            scratch_shapes=[
                pltpu.VMEM((row_tiles + 1, features, TILE), bf16),
                pltpu.VMEM((slots + 1, TILE, TILE), bf16),
                pltpu.VMEM((col_tiles, features, TILE), f32),
                pltpu.VMEM((CORES, 8, PANEL, features, TILE), bf16),
                pltpu.SemaphoreType.DMA((8,)),
                pltpu.SemaphoreType.DMA((slots // CHUNK,)),
                pltpu.SemaphoreType.DMA((CORES, 8)),
            ],
            compiler_params=pltpu.CompilerParams(vmem_limit_bytes=VMEM_BYTES),
            cost_estimate=tile_dots,
            name="column_gradients",
        )(meta, tile_cols, pairs, total, tile_values, *grads)

    def send(k):
        dx, dy = RELATIVE[k]
        return from_wide(pairs_sum[k], dx, -dy & 3, 0)

    def together(values, part):
        *values, part = lax.optimization_barrier((*values, part))
        return values, part

    with jax.named_scope("scatter_gradients"):
        part = part + from_narrow(part, 1, 0)
        swap, keep, part = lax.optimization_barrier((swap, keep, part))
        swapped = from_wide(swap, 0, 0, 1)
        part = part + sum(from_wide(part, dx, 0, dc) for dx, dc in ((0, 1), (1, 0), (1, 1)))
        pairs_sum = [
            (keep[k].astype(f32) + swapped[k].astype(f32)).astype(bf16) for k in range(8)
        ]
        pairs_sum, part = together(pairs_sum, part)
        column = {k: send(k) for k in STEPS[0]}
        part = part + sum(from_wide(part, 0, dy, 0) for dy in (1, 2, 3))
        sent, part = together([column[k] for k in STEPS[0]], part)
        column.update(zip(STEPS[0], sent))
        column.update((k, send(k)) for k in STEPS[1])
        quarters = [part] + [from_narrow(part, 0, dz) for dz in (1, 2, 3)]
        sent = lax.optimization_barrier([column[k] for k in STEPS[1]] + quarters)
        column.update(zip(STEPS[1], sent))
        quarters = sent[len(STEPS[1]) :]
        column.update((k, send(k)) for k in STEPS[2])

    with jax.named_scope("grad_input"):
        slice_spec = pl.BlockSpec((SLICE + 8, hidden), lambda i: (0, 0))
        first_spec = pl.BlockSpec((1, block // TILE, features, TILE), lambda i: (0, i, 0, 0))
        grad_input, grad_self, grad_neigh, grad_bias = pl.pallas_call(
            final_kernel,
            grid=(own_nodes // block,),
            out_shape=[
                jax.ShapeDtypeStruct((own_nodes, features), bf16),
                jax.ShapeDtypeStruct((features, hidden), f32),
                jax.ShapeDtypeStruct((features, hidden), f32),
                jax.ShapeDtypeStruct((1, hidden), f32),
            ],
            in_specs=[smem, first_spec, first_spec]
            + [piece_spec] * 7
            + [node_spec]
            + [slice_spec] * Z,
            out_specs=[
                node_spec,
                weight_spec,
                weight_spec,
                pl.BlockSpec((1, hidden), lambda i: (0, 0)),
            ],
            compiler_params=pltpu.CompilerParams(vmem_limit_bytes=VMEM_BYTES),
            name="grad_input",
        )(meta, keep, swapped, *[column[k] for k in range(1, 8)], self_term, *quarters)
    return (output, grad_input, grad_self, grad_neigh, grad_bias[0])


def solution(mesh):
    placed = (
        P(("wide", "narrow"), None),
        P(("wide", "narrow"), None, None),
        P(("wide", "narrow")),
        P(("wide", "narrow")),
        P(("wide", "narrow")),
        P(),
        P(),
        P(),
        P(("wide", "narrow"), None),
    )
    return jax.shard_map(
        local,
        mesh=mesh,
        in_specs=placed,
        out_specs=(P(("wide", "narrow"), None), P(("wide", "narrow"), None), P(), P(), P()),
        check_vma=False,
    )
```

```python
import jax
import jax.numpy as jnp
from jax import lax
from jax.experimental import pallas as pl
from jax.experimental.pallas import tpu as pltpu
from jax.sharding import PartitionSpec as P

TILE = 128
X_LO, Y, CORES = 2, 4, 2
X_HI, Z = 2, 4
PANEL = 8
CHUNK = 32
UNROLL = 32
BATCH = 4
SLICE = 64
STEPS = ((), (4, 6, 2), (1, 3, 5, 7))
VMEM_BYTES = 36 * 1024 * 1024
SMALL_BYTES = 16 * 1024 * 1024
RELATIVE = [(dx, dy) for dx in (0, 1) for dy in range(4)]


def wide_index(w, dx, dy, dc):
    return ((w >> 3) ^ dx) * 8 + ((((w >> 1) & 3) + dy) & 3) * 2 + ((w & 1) ^ dc)


def narrow_index(n, dx, dz):
    return ((n >> 2) ^ dx) * 4 + (((n & 3) + dz) & 3)


def from_wide(x, dx, dy, dc):
    return lax.ppermute(x, "wide", [(wide_index(w, dx, dy, dc), w) for w in range(16)])


def from_narrow(x, dx, dz):
    return lax.ppermute(x, "narrow", [(narrow_index(n, dx, dz), n) for n in range(8)])


def gather_ring(x, fetch, together):
    first = [(1, 0), (0, 2), (0, 1), (0, 3)]
    got = dict(zip(first, together([fetch(x, *key) for key in first])))
    got[0, 0] = x
    got[1, 1] = fetch(got[1, 0], 0, 1)
    got[1, 3] = fetch(got[1, 0], 0, 3)
    got[1, 2] = fetch(got[0, 2], 1, 0)
    return [got[key] for key in RELATIVE]


def load_tiles(tiles_hbm, tiles, sems, count):
    chunks = tiles_hbm.shape[0] // CHUNK
    copies = [
        pltpu.make_async_copy(
            tiles_hbm.at[pl.ds(k * CHUNK, CHUNK)], tiles.at[pl.ds(k * CHUNK, CHUNK)], sems.at[k]
        )
        for k in range(chunks)
    ]
    for k, copy in enumerate(copies):

        @pl.when(k * CHUNK < count)
        def _():
            copy.start()


def wait_chunk(tiles_hbm, tiles, sems, k):
    span = pl.ds(k * CHUNK, CHUNK)
    pltpu.make_async_copy(tiles_hbm.at[span], tiles.at[span], sems.at[k]).wait()


def plan_kernel(meta, rows, pairs, total):
    slots, trash = rows.shape[0], meta[3]
    count = meta[0]

    def place(state):
        s, k = state
        row = rows[s]
        after = jnp.minimum(s + 1, slots - 1)
        both = (s + 1 < count) & (rows[after] == row)
        pairs[0, k] = row
        pairs[1, k] = s
        pairs[2, k] = jnp.where(both, s + 1, slots)
        return s + 1 + both.astype(jnp.int32), k + 1

    _, k = lax.while_loop(lambda state: state[0] < count, place, (jnp.int32(0), jnp.int32(0)))
    total[0] = (k + UNROLL - 1) // UNROLL
    for u in range(UNROLL):
        pairs[0, k + u] = trash
        pairs[1, k + u] = slots
        pairs[2, k + u] = slots


def visit_pairs(count, total, pairs, visit, tiles_hbm, tiles, sems):
    last = (count + CHUNK - 1) // CHUNK - 1

    def group(i, arrived):
        needed = jnp.minimum((pairs[1, i * UNROLL + UNROLL - 1] + 1) // CHUNK, last)

        def wait(k, carry):
            wait_chunk(tiles_hbm, tiles, sems, k)
            return carry

        lax.fori_loop(arrived, needed + 1, wait, 0)
        visit([[pairs[j, i * UNROLL + u] for j in range(3)] for u in range(UNROLL)])
        return needed + 1

    lax.fori_loop(0, total[0], group, jnp.int32(0))


def forward_kernel(meta, cols, pairs, total, tiles_hbm, *refs):
    panels_hbm, outs = refs[:16], refs[16:24]
    panels, tiles, acc, staged, panel_sems, tile_sems, out_sems = refs[24:]
    count, w, n = meta[0], meta[1], meta[2]
    copies = []
    for k in range(16):
        dx, dy = RELATIVE[k % 8]
        owner = wide_index(w, dx, dy, k // 8)
        copies.append(
            pltpu.make_async_copy(
                panels_hbm[k], panels.at[pl.ds(owner * 1024, 1024)], panel_sems.at[k]
            )
        )
    for copy in copies:
        copy.start()
    load_tiles(tiles_hbm, tiles, tile_sems, count)
    acc[...] = jnp.zeros_like(acc)
    tiles[tiles.shape[0] - 1] = jnp.zeros(tiles.shape[1:], tiles.dtype)
    for copy in copies:
        copy.wait()

    def panel(s):
        column = pl.multiple_of(cols[jnp.minimum(s, cols.shape[0] - 1)] * TILE, TILE)
        return panels[pl.ds(column, TILE), :]

    def visit(group):
        for part in range(0, UNROLL, BATCH):
            products = []
            for row, first, second in group[part : part + BATCH]:
                left = jnp.concatenate([tiles[first], tiles[second]], axis=1)
                right = jnp.concatenate([panel(first), panel(second)], axis=0)
                products.append(jnp.dot(left, right, preferred_element_type=jnp.float32))
            for (row, _, _), product in zip(group[part : part + BATCH], products):
                acc[row] += product

    visit_pairs(count, total, pairs, visit, tiles_hbm, tiles, tile_sems)
    for k, (dx, dz) in enumerate(RELATIVE):
        owner = narrow_index(n, dx, dz)
        block = acc[pl.ds(owner * PANEL, PANEL)]
        staged[k] = block.reshape(PANEL * TILE, -1).astype(jnp.bfloat16)
        pltpu.make_async_copy(staged.at[k], outs[k], out_sems.at[k]).start()
    for k in range(8):
        pltpu.make_async_copy(staged.at[k], outs[k], out_sems.at[k]).wait()


def dense_kernel(
    own, r1, r2, r3, r4, r5, r6, r7, x, ws, wn, bias, grad, output, agg_out, pre_out, back_out
):
    agg = own[...].astype(jnp.float32)
    for r in (r1, r2, r3, r4, r5, r6, r7):
        agg = agg + r[...].astype(jnp.float32)
    agg = agg.astype(jnp.bfloat16)
    agg_out[...] = agg
    preact = jnp.dot(x[...], ws[...], preferred_element_type=jnp.float32)
    preact = preact + jnp.dot(agg, wn[...], preferred_element_type=jnp.float32) + bias[...]
    sigma = jax.nn.sigmoid(preact)
    output[...] = (preact * sigma).astype(jnp.bfloat16)
    pre = grad[...].astype(jnp.float32) * sigma * (1.0 + preact * (1.0 - sigma))
    pre = pre.astype(jnp.bfloat16)
    pre_out[...] = pre
    back = lax.dot_general(
        wn[...], pre, (((1,), (1,)), ((), ())), preferred_element_type=jnp.float32
    )
    back = back.astype(jnp.bfloat16)
    for k in range(back_out.shape[0]):
        back_out[k] = back[:, k * TILE : (k + 1) * TILE]


def weight_kernel(scale, meta, x, agg, pre, ws, slices, self_term):
    rows = (((0,), (0,)), ((), ()))
    n = meta[2]
    block = pre[...]
    total = scale * jnp.sum(block.astype(jnp.float32), axis=0, keepdims=True)
    total = jnp.broadcast_to(total, (8, total.shape[1]))
    for j, left in enumerate((x, agg)):
        grads = scale * lax.dot_general(left[...], block, rows, preferred_element_type=jnp.float32)
        for k in range(2):
            place = (2 * j + k - n) & 3
            slices[place, :SLICE] = grads[k * SLICE : (k + 1) * SLICE]
            slices[place, SLICE:] = total
    self_term[...] = lax.dot_general(
        block, ws[...], (((1,), (1,)), ((), ())), preferred_element_type=jnp.float32
    )


def backward_kernel(meta, cols, pairs, total, tiles_hbm, *refs):
    grads_hbm, (swap, keep) = refs[:8], refs[8:10]
    grads, tiles, acc, staged, grad_sems, tile_sems, out_sems = refs[10:]
    count, w, n = meta[0], meta[1], meta[2]
    copies = []
    for k, (dx, dz) in enumerate(RELATIVE):
        owner = narrow_index(n, dx, dz)
        copies.append(
            pltpu.make_async_copy(
                grads_hbm[k], grads.at[pl.ds(owner * PANEL, PANEL)], grad_sems.at[k]
            )
        )
    for copy in copies:
        copy.start()
    load_tiles(tiles_hbm, tiles, tile_sems, count)
    acc[...] = jnp.zeros_like(acc)
    tiles[tiles.shape[0] - 1] = jnp.zeros(tiles.shape[1:], tiles.dtype)
    grads[grads.shape[0] - 1] = jnp.zeros(grads.shape[1:], grads.dtype)
    for copy in copies:
        copy.wait()

    def visit(group):
        for part in range(0, UNROLL, BATCH):
            products = []
            for row, first, second in group[part : part + BATCH]:
                right = jnp.concatenate([tiles[first], tiles[second]], axis=1)
                products.append(jnp.dot(grads[row], right, preferred_element_type=jnp.float32))
            for (_, first, second), product in zip(group[part : part + BATCH], products):
                last = cols.shape[0] - 1
                acc[cols[jnp.minimum(first, last)]] += product[:, :TILE]
                acc[cols[jnp.minimum(second, last)]] += product[:, TILE:]

    visit_pairs(count, total, pairs, visit, tiles_hbm, tiles, tile_sems)
    outs = ((1, swap), (0, keep))
    for dc, out in outs:
        for k, (dx, dy) in enumerate(RELATIVE):
            owner = wide_index(w, dx, dy, dc)
            staged[dc, k] = acc[pl.ds(owner * PANEL, PANEL)].astype(jnp.bfloat16)
            pltpu.make_async_copy(staged.at[dc, k], out.at[k], out_sems.at[dc, k]).start()
    for dc, out in outs:
        for k in range(8):
            pltpu.make_async_copy(staged.at[dc, k], out.at[k], out_sems.at[dc, k]).wait()


def final_kernel(
    meta, keep, swapped, r1, r2, r3, r4, r5, r6, r7, self_term, s0, s1, s2, s3, *outs
):
    out, grad_self, grad_neigh, grad_bias = outs
    for j in range(r1.shape[0]):
        total = keep[0, j].astype(jnp.float32) + swapped[0, j].astype(jnp.float32)
        for r in (r1, r2, r3, r4, r5, r6, r7):
            total = total + r[j].astype(jnp.float32)
        rows = pl.ds(j * TILE, TILE)
        out[rows, :] = (self_term[rows, :] + total.T).astype(jnp.bfloat16)

    @pl.when(pl.program_id(0) == 0)
    def _():
        grad_bias[...] = s0[SLICE : SLICE + 1, :]
        for dz, s in enumerate((s0, s1, s2, s3)):
            place = (meta[2] + dz) & 3
            rows = pl.ds(pl.multiple_of((place & 1) * SLICE, SLICE), SLICE)

            @pl.when(place < 2)
            def _():
                grad_self[rows, :] = s[:SLICE, :]

            @pl.when(place >= 2)
            def _():
                grad_neigh[rows, :] = s[:SLICE, :]


def local(
    node_features,
    tile_values,
    tile_rows,
    tile_cols,
    tile_count,
    weight_self,
    weight_neigh,
    bias_vector,
    grad_output,
):
    slots = tile_values.shape[0]
    own_nodes, features = node_features.shape
    hidden = weight_self.shape[1]
    wide_count = lax.axis_size("wide")
    narrow_count = lax.axis_size("narrow")
    row_tiles = narrow_count * PANEL
    col_tiles = wide_count * PANEL
    w, n = lax.axis_index("wide"), lax.axis_index("narrow")
    meta = jnp.stack([tile_count[0], w.astype(jnp.int32), n.astype(jnp.int32), row_tiles])
    smem = pl.BlockSpec(memory_space=pltpu.SMEM)
    hbm = pl.BlockSpec(memory_space=pl.ANY)
    vmem = pl.BlockSpec(memory_space=pltpu.VMEM)
    scale = float(own_nodes * wide_count * narrow_count) ** (-0.5)
    bf16, f32 = jnp.bfloat16, jnp.float32
    tile_dots = pl.CostEstimate(
        flops=2 * slots * TILE * TILE * features,
        bytes_accessed=2 * slots * TILE * TILE + 6 * 1024 * 1024,
        transcendentals=0,
    )

    with jax.named_scope("plan"):
        pairs, total = pl.pallas_call(
            plan_kernel,
            out_shape=[
                jax.ShapeDtypeStruct((3, (slots + row_tiles) // 2 + UNROLL), jnp.int32),
                jax.ShapeDtypeStruct((1,), jnp.int32),
            ],
            in_specs=[smem] * 2,
            out_specs=[smem] * 2,
            name="plan",
        )(meta, tile_rows)

    def after_plan(blocks):
        return lax.optimization_barrier((*blocks, total))[:-1]

    with jax.named_scope("gather_features"):
        same_core = gather_ring(
            node_features, lambda v, dx, dy: from_wide(v, dx, dy, 0), after_plan
        )
        other_core = [from_wide(v, 0, 0, 1) for v in same_core]

    with jax.named_scope("aggregate"):
        partial = pl.pallas_call(
            forward_kernel,
            out_shape=[jax.ShapeDtypeStruct((own_nodes, features), bf16)] * 8,
            in_specs=[smem] * 4 + [hbm] * 17,
            out_specs=[hbm] * 8,
            scratch_shapes=[
                pltpu.VMEM((col_tiles * TILE, features), bf16),
                pltpu.VMEM((slots + 1, TILE, TILE), bf16),
                pltpu.VMEM((row_tiles + 1, TILE, features), f32),
                pltpu.VMEM((8, own_nodes, features), bf16),
                pltpu.SemaphoreType.DMA((16,)),
                pltpu.SemaphoreType.DMA((slots // CHUNK,)),
                pltpu.SemaphoreType.DMA((8,)),
            ],
            compiler_params=pltpu.CompilerParams(vmem_limit_bytes=VMEM_BYTES),
            cost_estimate=tile_dots,
            name="aggregate",
        )(meta, tile_cols, pairs, total, tile_values, *same_core, *other_core)

    with jax.named_scope("scatter_aggregate"):
        received = [from_narrow(partial[k], RELATIVE[k][0], -k & 3) for k in (6, 4, 2, 5, 7, 1, 3)]

    block = own_nodes // 2
    node_spec = pl.BlockSpec((block, features), lambda i: (i, 0))
    hid_spec = pl.BlockSpec((block, hidden), lambda i: (i, 0))
    weight_spec = pl.BlockSpec((features, hidden), lambda i: (0, 0))
    piece_spec = pl.BlockSpec((block // TILE, features, TILE), lambda i: (i, 0, 0))
    with jax.named_scope("dense"):
        output, own_agg, grad_pre, back = pl.pallas_call(
            dense_kernel,
            grid=(own_nodes // block,),
            out_shape=[
                jax.ShapeDtypeStruct((own_nodes, hidden), bf16),
                jax.ShapeDtypeStruct((own_nodes, features), bf16),
                jax.ShapeDtypeStruct((own_nodes, hidden), bf16),
                jax.ShapeDtypeStruct((PANEL, features, TILE), bf16),
            ],
            in_specs=[node_spec] * 9
            + [weight_spec, weight_spec, pl.BlockSpec((1, hidden), lambda i: (0, 0)), hid_spec],
            out_specs=[hid_spec, node_spec, hid_spec, piece_spec],
            compiler_params=pltpu.CompilerParams(vmem_limit_bytes=SMALL_BYTES),
            name="dense",
        )(
            partial[0],
            *received,
            node_features,
            weight_self,
            weight_neigh,
            bias_vector.reshape(1, hidden),
            grad_output,
        )

    with jax.named_scope("weight_gradients"):
        slices, self_term = pl.pallas_call(
            lambda *refs: weight_kernel(scale, *refs),
            out_shape=[
                jax.ShapeDtypeStruct((Z, SLICE + 8, hidden), f32),
                jax.ShapeDtypeStruct((own_nodes, features), f32),
            ],
            in_specs=[smem] + [vmem] * 4,
            out_specs=[vmem] * 2,
            compiler_params=pltpu.CompilerParams(vmem_limit_bytes=SMALL_BYTES),
            cost_estimate=pl.CostEstimate(
                flops=6 * own_nodes * features * hidden,
                bytes_accessed=2 * 1024 * 1024,
                transcendentals=0,
            ),
            name="weight_gradients",
        )(meta, node_features, own_agg, grad_pre, weight_self)

        part = slices[0] + sum(from_narrow(slices[dz], 0, -dz & 3) for dz in (1, 2, 3))

    with jax.named_scope("gather_gradients"):
        grads = gather_ring(back, from_narrow, lax.optimization_barrier)
        *grads, part = lax.optimization_barrier((*grads, part))

    with jax.named_scope("column_gradients"):
        pieces = jax.ShapeDtypeStruct((8, PANEL, features, TILE), bf16)
        swap, keep = pl.pallas_call(
            backward_kernel,
            out_shape=[pieces, pieces],
            in_specs=[smem] * 4 + [hbm] * 9,
            out_specs=[hbm] * 2,
            scratch_shapes=[
                pltpu.VMEM((row_tiles + 1, features, TILE), bf16),
                pltpu.VMEM((slots + 1, TILE, TILE), bf16),
                pltpu.VMEM((col_tiles, features, TILE), f32),
                pltpu.VMEM((CORES, 8, PANEL, features, TILE), bf16),
                pltpu.SemaphoreType.DMA((8,)),
                pltpu.SemaphoreType.DMA((slots // CHUNK,)),
                pltpu.SemaphoreType.DMA((CORES, 8)),
            ],
            compiler_params=pltpu.CompilerParams(vmem_limit_bytes=VMEM_BYTES),
            cost_estimate=tile_dots,
            name="column_gradients",
        )(meta, tile_cols, pairs, total, tile_values, *grads)

    def send(k):
        dx, dy = RELATIVE[k]
        return from_wide(pairs_sum[k], dx, -dy & 3, 0)

    def together(values, part):
        *values, part = lax.optimization_barrier((*values, part))
        return values, part

    with jax.named_scope("scatter_gradients"):
        part = part + from_narrow(part, 1, 0)
        swap, keep, part = lax.optimization_barrier((swap, keep, part))
        swapped = from_wide(swap, 0, 0, 1)
        part = part + sum(from_wide(part, dx, 0, dc) for dx, dc in ((0, 1), (1, 0), (1, 1)))
        pairs_sum = [
            (keep[k].astype(f32) + swapped[k].astype(f32)).astype(bf16) for k in range(8)
        ]
        pairs_sum, part = together(pairs_sum, part)
        column = {k: send(k) for k in STEPS[0]}
        part = part + sum(from_wide(part, 0, dy, 0) for dy in (1, 2, 3))
        sent, part = together([column[k] for k in STEPS[0]], part)
        column.update(zip(STEPS[0], sent))
        column.update((k, send(k)) for k in STEPS[1])
        quarters = [part] + [from_narrow(part, 0, dz) for dz in (1, 2, 3)]
        sent = lax.optimization_barrier([column[k] for k in STEPS[1]] + quarters)
        column.update(zip(STEPS[1], sent))
        quarters = sent[len(STEPS[1]) :]
        column.update((k, send(k)) for k in STEPS[2])

    with jax.named_scope("grad_input"):
        slice_spec = pl.BlockSpec((SLICE + 8, hidden), lambda i: (0, 0))
        first_spec = pl.BlockSpec((1, block // TILE, features, TILE), lambda i: (0, i, 0, 0))
        grad_input, grad_self, grad_neigh, grad_bias = pl.pallas_call(
            final_kernel,
            grid=(own_nodes // block,),
            out_shape=[
                jax.ShapeDtypeStruct((own_nodes, features), bf16),
                jax.ShapeDtypeStruct((features, hidden), f32),
                jax.ShapeDtypeStruct((features, hidden), f32),
                jax.ShapeDtypeStruct((1, hidden), f32),
            ],
            in_specs=[smem, first_spec, first_spec]
            + [piece_spec] * 7
            + [node_spec]
            + [slice_spec] * Z,
            out_specs=[
                node_spec,
                weight_spec,
                weight_spec,
                pl.BlockSpec((1, hidden), lambda i: (0, 0)),
            ],
            compiler_params=pltpu.CompilerParams(vmem_limit_bytes=SMALL_BYTES),
            name="grad_input",
        )(meta, keep, swapped, *[column[k] for k in range(1, 8)], self_term, *quarters)
    return (output, grad_input, grad_self, grad_neigh, grad_bias[0])


def solution(mesh):
    placed = (
        P(("wide", "narrow"), None),
        P(("wide", "narrow"), None, None),
        P(("wide", "narrow")),
        P(("wide", "narrow")),
        P(("wide", "narrow")),
        P(),
        P(),
        P(),
        P(("wide", "narrow"), None),
    )
    return jax.shard_map(
        local,
        mesh=mesh,
        in_specs=placed,
        out_specs=(P(("wide", "narrow"), None), P(("wide", "narrow"), None), P(), P(), P()),
        check_vma=False,
    )
```

```python
import jax
import jax.numpy as jnp
from jax import lax
from jax.experimental import pallas as pl
from jax.experimental.pallas import tpu as pltpu
from jax.sharding import PartitionSpec as P

TILE = 128
X_LO, Y, CORES = 2, 4, 2
X_HI, Z = 2, 4
PANEL = 8
CHUNK = 32
UNROLL = 32
BATCH = 4
SLICE = 64
STEPS = ((), (4, 6, 2), (1, 3, 5, 7))
VMEM_BYTES = 36 * 1024 * 1024
SMALL_BYTES = 16 * 1024 * 1024
RELATIVE = [(dx, dy) for dx in (0, 1) for dy in range(4)]


def wide_index(w, dx, dy, dc):
    return ((w >> 3) ^ dx) * 8 + ((((w >> 1) & 3) + dy) & 3) * 2 + ((w & 1) ^ dc)


def narrow_index(n, dx, dz):
    return ((n >> 2) ^ dx) * 4 + (((n & 3) + dz) & 3)


def from_wide(x, dx, dy, dc):
    return lax.ppermute(x, "wide", [(wide_index(w, dx, dy, dc), w) for w in range(16)])


def from_narrow(x, dx, dz):
    return lax.ppermute(x, "narrow", [(narrow_index(n, dx, dz), n) for n in range(8)])


def gather_ring(x, fetch, together):
    first = [(1, 0), (0, 2), (0, 1), (0, 3)]
    got = dict(zip(first, together([fetch(x, *key) for key in first])))
    got[0, 0] = x
    got[1, 1] = fetch(got[1, 0], 0, 1)
    got[1, 3] = fetch(got[1, 0], 0, 3)
    got[1, 2] = fetch(got[0, 2], 1, 0)
    return [got[key] for key in RELATIVE]


def load_tiles(tiles_hbm, tiles, sems, count):
    chunks = tiles_hbm.shape[0] // CHUNK
    copies = [
        pltpu.make_async_copy(
            tiles_hbm.at[pl.ds(k * CHUNK, CHUNK)], tiles.at[pl.ds(k * CHUNK, CHUNK)], sems.at[k]
        )
        for k in range(chunks)
    ]
    for k, copy in enumerate(copies):

        @pl.when(k * CHUNK < count)
        def _():
            copy.start()


def wait_chunk(tiles_hbm, tiles, sems, k):
    span = pl.ds(k * CHUNK, CHUNK)
    pltpu.make_async_copy(tiles_hbm.at[span], tiles.at[span], sems.at[k]).wait()


def plan_kernel(meta, rows, pairs, total):
    slots, trash = rows.shape[0], meta[3]
    count = meta[0]

    def place(state):
        s, k = state
        row = rows[s]
        after = jnp.minimum(s + 1, slots - 1)
        both = (s + 1 < count) & (rows[after] == row)
        pairs[0, k] = row
        pairs[1, k] = s
        pairs[2, k] = jnp.where(both, s + 1, slots)
        return s + 1 + both.astype(jnp.int32), k + 1

    _, k = lax.while_loop(lambda state: state[0] < count, place, (jnp.int32(0), jnp.int32(0)))
    total[0] = (k + UNROLL - 1) // UNROLL
    for u in range(UNROLL):
        pairs[0, k + u] = trash
        pairs[1, k + u] = slots
        pairs[2, k + u] = slots


def visit_pairs(count, total, pairs, visit, tiles_hbm, tiles, sems):
    last = (count + CHUNK - 1) // CHUNK - 1

    def group(i, arrived):
        needed = jnp.minimum((pairs[1, i * UNROLL + UNROLL - 1] + 1) // CHUNK, last)

        def wait(k, carry):
            wait_chunk(tiles_hbm, tiles, sems, k)
            return carry

        lax.fori_loop(arrived, needed + 1, wait, 0)
        visit([[pairs[j, i * UNROLL + u] for j in range(3)] for u in range(UNROLL)])
        return needed + 1

    lax.fori_loop(0, total[0], group, jnp.int32(0))


def forward_kernel(meta, cols, pairs, total, tiles_hbm, *refs):
    panels_hbm, outs = refs[:16], refs[16:24]
    panels, tiles, acc, staged, panel_sems, tile_sems, out_sems = refs[24:]
    count, w, n = meta[0], meta[1], meta[2]
    copies = []
    for k in range(16):
        dx, dy = RELATIVE[k % 8]
        owner = wide_index(w, dx, dy, k // 8)
        copies.append(
            pltpu.make_async_copy(
                panels_hbm[k], panels.at[pl.ds(owner * 1024, 1024)], panel_sems.at[k]
            )
        )
    for copy in copies:
        copy.start()
    load_tiles(tiles_hbm, tiles, tile_sems, count)
    acc[...] = jnp.zeros_like(acc)
    tiles[tiles.shape[0] - 1] = jnp.zeros(tiles.shape[1:], tiles.dtype)
    for copy in copies:
        copy.wait()

    def panel(s):
        column = pl.multiple_of(cols[jnp.minimum(s, cols.shape[0] - 1)] * TILE, TILE)
        return panels[pl.ds(column, TILE), :]

    def visit(group):
        for part in range(0, UNROLL, BATCH):
            products = []
            for row, first, second in group[part : part + BATCH]:
                left = jnp.concatenate([tiles[first], tiles[second]], axis=1)
                right = jnp.concatenate([panel(first), panel(second)], axis=0)
                products.append(jnp.dot(left, right, preferred_element_type=jnp.float32))
            for (row, _, _), product in zip(group[part : part + BATCH], products):
                acc[row] += product

    visit_pairs(count, total, pairs, visit, tiles_hbm, tiles, tile_sems)
    for k, (dx, dz) in enumerate(RELATIVE):
        owner = narrow_index(n, dx, dz)
        block = acc[pl.ds(owner * PANEL, PANEL)]
        staged[k] = block.reshape(PANEL * TILE, -1).astype(jnp.bfloat16)
        pltpu.make_async_copy(staged.at[k], outs[k], out_sems.at[k]).start()
    for k in range(8):
        pltpu.make_async_copy(staged.at[k], outs[k], out_sems.at[k]).wait()


def dense_kernel(
    own, r1, r2, r3, r4, r5, r6, r7, x, ws, wn, bias, grad, output, agg_out, pre_out, back_out
):
    agg = own[...].astype(jnp.float32)
    for r in (r1, r2, r3, r4, r5, r6, r7):
        agg = agg + r[...].astype(jnp.float32)
    agg = agg.astype(jnp.bfloat16)
    agg_out[...] = agg
    preact = jnp.dot(x[...], ws[...], preferred_element_type=jnp.float32)
    preact = preact + jnp.dot(agg, wn[...], preferred_element_type=jnp.float32) + bias[...]
    sigma = jax.nn.sigmoid(preact)
    output[...] = (preact * sigma).astype(jnp.bfloat16)
    pre = grad[...].astype(jnp.float32) * sigma * (1.0 + preact * (1.0 - sigma))
    pre = pre.astype(jnp.bfloat16)
    pre_out[...] = pre
    back = lax.dot_general(
        wn[...], pre, (((1,), (1,)), ((), ())), preferred_element_type=jnp.float32
    )
    back = back.astype(jnp.bfloat16)
    for k in range(back_out.shape[0]):
        back_out[k] = back[:, k * TILE : (k + 1) * TILE]


def weight_kernel(scale, meta, x, agg, pre, ws, slices, self_term):
    rows = (((0,), (0,)), ((), ()))
    n = meta[2]
    block = pre[...]
    total = scale * jnp.sum(block.astype(jnp.float32), axis=0, keepdims=True)
    total = jnp.broadcast_to(total, (8, total.shape[1]))
    for j, left in enumerate((x, agg)):
        grads = scale * lax.dot_general(left[...], block, rows, preferred_element_type=jnp.float32)
        for k in range(2):
            place = (2 * j + k - n) & 3
            slices[place, :SLICE] = grads[k * SLICE : (k + 1) * SLICE]
            slices[place, SLICE:] = total
    self_term[...] = lax.dot_general(
        block, ws[...], (((1,), (1,)), ((), ())), preferred_element_type=jnp.float32
    )


def backward_kernel(meta, cols, pairs, total, tiles_hbm, *refs):
    grads_hbm, (swap, keep) = refs[:8], refs[8:10]
    grads, tiles, acc, staged, grad_sems, tile_sems, out_sems = refs[10:]
    count, w, n = meta[0], meta[1], meta[2]
    copies = []
    for k, (dx, dz) in enumerate(RELATIVE):
        owner = narrow_index(n, dx, dz)
        copies.append(
            pltpu.make_async_copy(
                grads_hbm[k], grads.at[pl.ds(owner * PANEL, PANEL)], grad_sems.at[k]
            )
        )
    for copy in copies:
        copy.start()
    load_tiles(tiles_hbm, tiles, tile_sems, count)
    acc[...] = jnp.zeros_like(acc)
    tiles[tiles.shape[0] - 1] = jnp.zeros(tiles.shape[1:], tiles.dtype)
    grads[grads.shape[0] - 1] = jnp.zeros(grads.shape[1:], grads.dtype)
    for copy in copies:
        copy.wait()

    def visit(group):
        for part in range(0, UNROLL, BATCH):
            products = []
            for row, first, second in group[part : part + BATCH]:
                right = jnp.concatenate([tiles[first], tiles[second]], axis=1)
                products.append(jnp.dot(grads[row], right, preferred_element_type=jnp.float32))
            for (_, first, second), product in zip(group[part : part + BATCH], products):
                last = cols.shape[0] - 1
                acc[cols[jnp.minimum(first, last)]] += product[:, :TILE]
                acc[cols[jnp.minimum(second, last)]] += product[:, TILE:]

    visit_pairs(count, total, pairs, visit, tiles_hbm, tiles, tile_sems)
    outs = ((1, swap), (0, keep))
    for dc, out in outs:
        for k, (dx, dy) in enumerate(RELATIVE):
            owner = wide_index(w, dx, dy, dc)
            staged[dc, k] = acc[pl.ds(owner * PANEL, PANEL)].astype(jnp.bfloat16)
            pltpu.make_async_copy(staged.at[dc, k], out.at[k], out_sems.at[dc, k]).start()
    for dc, out in outs:
        for k in range(8):
            pltpu.make_async_copy(staged.at[dc, k], out.at[k], out_sems.at[dc, k]).wait()


def final_kernel(
    meta, keep, swapped, r1, r2, r3, r4, r5, r6, r7, self_term, s0, s1, s2, s3, *outs
):
    out, grad_self, grad_neigh, grad_bias = outs
    for j in range(r1.shape[0]):
        total = keep[0, j].astype(jnp.float32) + swapped[0, j].astype(jnp.float32)
        for r in (r1, r2, r3, r4, r5, r6, r7):
            total = total + r[j].astype(jnp.float32)
        rows = pl.ds(j * TILE, TILE)
        out[rows, :] = (self_term[rows, :] + total.T).astype(jnp.bfloat16)

    @pl.when(pl.program_id(0) == 0)
    def _():
        grad_bias[...] = s0[SLICE : SLICE + 1, :]
        for dz, s in enumerate((s0, s1, s2, s3)):
            place = (meta[2] + dz) & 3
            rows = pl.ds(pl.multiple_of((place & 1) * SLICE, SLICE), SLICE)

            @pl.when(place < 2)
            def _():
                grad_self[rows, :] = s[:SLICE, :]

            @pl.when(place >= 2)
            def _():
                grad_neigh[rows, :] = s[:SLICE, :]


def local(
    node_features,
    tile_values,
    tile_rows,
    tile_cols,
    tile_count,
    weight_self,
    weight_neigh,
    bias_vector,
    grad_output,
):
    slots = tile_values.shape[0]
    own_nodes, features = node_features.shape
    hidden = weight_self.shape[1]
    wide_count = lax.axis_size("wide")
    narrow_count = lax.axis_size("narrow")
    row_tiles = narrow_count * PANEL
    col_tiles = wide_count * PANEL
    w, n = lax.axis_index("wide"), lax.axis_index("narrow")
    meta = jnp.stack([tile_count[0], w.astype(jnp.int32), n.astype(jnp.int32), row_tiles])
    smem = pl.BlockSpec(memory_space=pltpu.SMEM)
    hbm = pl.BlockSpec(memory_space=pl.ANY)
    vmem = pl.BlockSpec(memory_space=pltpu.VMEM)
    scale = float(own_nodes * wide_count * narrow_count) ** (-0.5)
    bf16, f32 = jnp.bfloat16, jnp.float32
    tile_dots = pl.CostEstimate(
        flops=2 * slots * TILE * TILE * features,
        bytes_accessed=2 * slots * TILE * TILE + 6 * 1024 * 1024,
        transcendentals=0,
    )

    with jax.named_scope("plan"):
        pairs, total = pl.pallas_call(
            plan_kernel,
            out_shape=[
                jax.ShapeDtypeStruct((3, (slots + row_tiles) // 2 + UNROLL), jnp.int32),
                jax.ShapeDtypeStruct((1,), jnp.int32),
            ],
            in_specs=[smem] * 2,
            out_specs=[smem] * 2,
            name="plan",
        )(meta, tile_rows)

    def after_plan(blocks):
        return lax.optimization_barrier((*blocks, total))[:-1]

    with jax.named_scope("gather_features"):
        same_core = gather_ring(
            node_features, lambda v, dx, dy: from_wide(v, dx, dy, 0), after_plan
        )
        other_core = [from_wide(v, 0, 0, 1) for v in same_core]

    with jax.named_scope("aggregate"):
        partial = pl.pallas_call(
            forward_kernel,
            out_shape=[jax.ShapeDtypeStruct((own_nodes, features), bf16)] * 8,
            in_specs=[smem] * 4 + [hbm] * 17,
            out_specs=[hbm] * 8,
            scratch_shapes=[
                pltpu.VMEM((col_tiles * TILE, features), bf16),
                pltpu.VMEM((slots + 1, TILE, TILE), bf16),
                pltpu.VMEM((row_tiles + 1, TILE, features), f32),
                pltpu.VMEM((8, own_nodes, features), bf16),
                pltpu.SemaphoreType.DMA((16,)),
                pltpu.SemaphoreType.DMA((slots // CHUNK,)),
                pltpu.SemaphoreType.DMA((8,)),
            ],
            compiler_params=pltpu.CompilerParams(vmem_limit_bytes=VMEM_BYTES),
            cost_estimate=tile_dots,
            name="aggregate",
        )(meta, tile_cols, pairs, total, tile_values, *same_core, *other_core)

    with jax.named_scope("scatter_aggregate"):
        received = [from_narrow(partial[k], RELATIVE[k][0], -k & 3) for k in (6, 4, 2, 5, 7, 1, 3)]

    block = own_nodes // 2
    node_spec = pl.BlockSpec((block, features), lambda i: (i, 0))
    hid_spec = pl.BlockSpec((block, hidden), lambda i: (i, 0))
    weight_spec = pl.BlockSpec((features, hidden), lambda i: (0, 0))
    piece_spec = pl.BlockSpec((block // TILE, features, TILE), lambda i: (i, 0, 0))
    with jax.named_scope("dense"):
        output, own_agg, grad_pre, back = pl.pallas_call(
            dense_kernel,
            grid=(own_nodes // block,),
            out_shape=[
                jax.ShapeDtypeStruct((own_nodes, hidden), bf16),
                jax.ShapeDtypeStruct((own_nodes, features), bf16),
                jax.ShapeDtypeStruct((own_nodes, hidden), bf16),
                jax.ShapeDtypeStruct((PANEL, features, TILE), bf16),
            ],
            in_specs=[node_spec] * 9
            + [weight_spec, weight_spec, pl.BlockSpec((1, hidden), lambda i: (0, 0)), hid_spec],
            out_specs=[hid_spec, node_spec, hid_spec, piece_spec],
            compiler_params=pltpu.CompilerParams(vmem_limit_bytes=SMALL_BYTES),
            name="dense",
        )(
            partial[0],
            *received,
            node_features,
            weight_self,
            weight_neigh,
            bias_vector.reshape(1, hidden),
            grad_output,
        )

    with jax.named_scope("weight_gradients"):
        slices, self_term = pl.pallas_call(
            lambda *refs: weight_kernel(scale, *refs),
            out_shape=[
                jax.ShapeDtypeStruct((Z, SLICE + 8, hidden), f32),
                jax.ShapeDtypeStruct((own_nodes, features), f32),
            ],
            in_specs=[smem] + [vmem] * 4,
            out_specs=[vmem] * 2,
            compiler_params=pltpu.CompilerParams(vmem_limit_bytes=SMALL_BYTES),
            cost_estimate=pl.CostEstimate(
                flops=6 * own_nodes * features * hidden,
                bytes_accessed=2 * 1024 * 1024,
                transcendentals=0,
            ),
            name="weight_gradients",
        )(meta, node_features, own_agg, grad_pre, weight_self)

        sent = [from_narrow(slices[dz].astype(bf16), 0, -dz & 3) for dz in (1, 2, 3)]
        part = slices[0] + sum(v.astype(f32) for v in sent)

    with jax.named_scope("gather_gradients"):
        grads = gather_ring(back, from_narrow, lax.optimization_barrier)
        *grads, part = lax.optimization_barrier((*grads, part))

    with jax.named_scope("column_gradients"):
        pieces = jax.ShapeDtypeStruct((8, PANEL, features, TILE), bf16)
        swap, keep = pl.pallas_call(
            backward_kernel,
            out_shape=[pieces, pieces],
            in_specs=[smem] * 4 + [hbm] * 9,
            out_specs=[hbm] * 2,
            scratch_shapes=[
                pltpu.VMEM((row_tiles + 1, features, TILE), bf16),
                pltpu.VMEM((slots + 1, TILE, TILE), bf16),
                pltpu.VMEM((col_tiles, features, TILE), f32),
                pltpu.VMEM((CORES, 8, PANEL, features, TILE), bf16),
                pltpu.SemaphoreType.DMA((8,)),
                pltpu.SemaphoreType.DMA((slots // CHUNK,)),
                pltpu.SemaphoreType.DMA((CORES, 8)),
            ],
            compiler_params=pltpu.CompilerParams(vmem_limit_bytes=VMEM_BYTES),
            cost_estimate=tile_dots,
            name="column_gradients",
        )(meta, tile_cols, pairs, total, tile_values, *grads)

    def send(k):
        dx, dy = RELATIVE[k]
        return from_wide(pairs_sum[k], dx, -dy & 3, 0)

    def together(values, part):
        *values, part = lax.optimization_barrier((*values, part))
        return values, part

    with jax.named_scope("scatter_gradients"):
        part = part + from_narrow(part, 1, 0)
        swap, keep, part = lax.optimization_barrier((swap, keep, part))
        swapped = from_wide(swap, 0, 0, 1)
        part = part + sum(from_wide(part, dx, 0, dc) for dx, dc in ((0, 1), (1, 0), (1, 1)))
        pairs_sum = [
            (keep[k].astype(f32) + swapped[k].astype(f32)).astype(bf16) for k in range(8)
        ]
        pairs_sum, part = together(pairs_sum, part)
        column = {k: send(k) for k in STEPS[0]}
        part = part + sum(from_wide(part, 0, dy, 0) for dy in (1, 2, 3))
        sent, part = together([column[k] for k in STEPS[0]], part)
        column.update(zip(STEPS[0], sent))
        column.update((k, send(k)) for k in STEPS[1])
        quarters = [part] + [from_narrow(part, 0, dz) for dz in (1, 2, 3)]
        sent = lax.optimization_barrier([column[k] for k in STEPS[1]] + quarters)
        column.update(zip(STEPS[1], sent))
        quarters = sent[len(STEPS[1]) :]
        column.update((k, send(k)) for k in STEPS[2])

    with jax.named_scope("grad_input"):
        slice_spec = pl.BlockSpec((SLICE + 8, hidden), lambda i: (0, 0))
        first_spec = pl.BlockSpec((1, block // TILE, features, TILE), lambda i: (0, i, 0, 0))
        grad_input, grad_self, grad_neigh, grad_bias = pl.pallas_call(
            final_kernel,
            grid=(own_nodes // block,),
            out_shape=[
                jax.ShapeDtypeStruct((own_nodes, features), bf16),
                jax.ShapeDtypeStruct((features, hidden), f32),
                jax.ShapeDtypeStruct((features, hidden), f32),
                jax.ShapeDtypeStruct((1, hidden), f32),
            ],
            in_specs=[smem, first_spec, first_spec]
            + [piece_spec] * 7
            + [node_spec]
            + [slice_spec] * Z,
            out_specs=[
                node_spec,
                weight_spec,
                weight_spec,
                pl.BlockSpec((1, hidden), lambda i: (0, 0)),
            ],
            compiler_params=pltpu.CompilerParams(vmem_limit_bytes=SMALL_BYTES),
            name="grad_input",
        )(meta, keep, swapped, *[column[k] for k in range(1, 8)], self_term, *quarters)
    return (output, grad_input, grad_self, grad_neigh, grad_bias[0])


def solution(mesh):
    placed = (
        P(("wide", "narrow"), None),
        P(("wide", "narrow"), None, None),
        P(("wide", "narrow")),
        P(("wide", "narrow")),
        P(("wide", "narrow")),
        P(),
        P(),
        P(),
        P(("wide", "narrow"), None),
    )
    return jax.shard_map(
        local,
        mesh=mesh,
        in_specs=placed,
        out_specs=(P(("wide", "narrow"), None), P(("wide", "narrow"), None), P(), P(), P()),
        check_vma=False,
    )
```
